512 devices in a mesh: noise: 16 (over z_lo, x), dp: 32 (over z_hi, y, core).
Axes of the slice: x: 4, y: 8, z: 8 (z_hi: 2, z_lo: 4; z = z_hi * 4 + z_lo), core: 2. Of those that a mesh axis runs over, the one named last changes fastest.
Arguments:
- noise_latents: bfloat16 [2048, 65536], P('noise', 'dp'), as said below
- data_latents: bfloat16 [2048, 65536], P('noise', 'dp'), as said below
Outputs:
- targets: bfloat16 [2048, 65536], P('noise', 'dp')
- noise_potential: float32 [2048], P('noise')
- data_potential: float32 [2048], P('dp')
Inputs may be any that keep to these rules, and one draw needn't show every extreme that they name: `noise_latents`: any finite values. `data_latents`: any finite values.
All inputs are finite; a program needn't handle non-finite values.
Results may differ from the reference program's by a relative error of at most 0.002.
Values may be sent and summed in bfloat16 or wider, within the bound.
No kernel may reach another device: no remote copies, remote signals or barrier semaphores. Data moves between devices by JAX's collectives and lax.ppermute only.
A program may use at most 64 MiB of HBM per device.

```python
import math
import jax
import jax.numpy as jnp
from jax import lax

F = 65536
ITERS = 4
NN = 2048
ND = 2048


cluster_count = 8


center_weight = 0.6


own_weight = 0.8


aligned_pct = 12


def entries(key, bound):
    return jnp.clip(jax.random.normal(key, (F,), jnp.float32), -bound, bound)


def base_row(shared, index, bound, scale_lo, scale_hi):
    row_key = jax.random.fold_in(jax.random.fold_in(shared, 1), index)
    cluster = jax.random.randint(jax.random.fold_in(row_key, 1), (), 0, cluster_count)
    center = entries(jax.random.fold_in(jax.random.fold_in(shared, 2), cluster), bound)
    own = entries(jax.random.fold_in(row_key, 2), bound)
    spread = jnp.exp(jax.random.uniform(jax.random.fold_in(row_key, 3), (), jnp.float32, math.log(scale_lo), math.log(scale_hi)))
    return spread * (center_weight * center + own_weight * own)


def twin_flag(shared, couple, twin_pct):
    couple_key = jax.random.fold_in(jax.random.fold_in(shared, 3), couple)
    return jax.random.randint(jax.random.fold_in(couple_key, 1), (), 0, 100) < twin_pct


def data_row(shared, index, bound, scale_lo, scale_hi, twin_pct):
    couple = index // 2
    couple_key = jax.random.fold_in(jax.random.fold_in(shared, 3), couple)
    anchor = base_row(shared, 2 * couple, bound, scale_lo, scale_hi)
    own_row = base_row(shared, index, bound, scale_lo, scale_hi)
    distance = jax.random.uniform(jax.random.fold_in(couple_key, 2), (), jnp.float32, 0.01, 0.03)
    offset = entries(jax.random.fold_in(couple_key, 3), 4.0)
    near_copy = anchor + jnp.sqrt(distance) * offset
    use_copy = jnp.logical_and(index % 2 == 1, twin_flag(shared, couple, twin_pct))
    return jnp.where(use_copy, near_copy, own_row)


def draw_data_latents(key, part):
    bound, scale_lo, scale_hi, twin_pct = (4.0, 0.4, 2.5, 0)

    def one_row(index):
        return data_row(key, index, bound, scale_lo, scale_hi, twin_pct)
    rows = lax.map(one_row, jnp.arange(ND, dtype=jnp.int32))
    return rows.astype(jnp.bfloat16)


def draw_noise_latents(key, part):
    bound, scale_lo, scale_hi, twin_pct = (4.0, 0.4, 2.5, 0)
    exact_pct, strength_lo, strength_hi = (0, 0.5, 0.9)
    shared = key
    key = jax.random.fold_in(key, 11)
    chosen = jax.random.randint(jax.random.fold_in(key, 1), (), 0, NN // 2)

    def flag_of(couple):
        return twin_flag(shared, couple, twin_pct)
    twinned = jax.vmap(flag_of)(jnp.arange(ND // 2, dtype=jnp.int32)).astype(jnp.int32)

    def one_row(index):
        row_key = jax.random.fold_in(jax.random.fold_in(key, 2), index)
        couple_key = jax.random.fold_in(jax.random.fold_in(key, 3), index // 2)
        own = entries(jax.random.fold_in(row_key, 1), bound)
        spread = jnp.exp(jax.random.uniform(jax.random.fold_in(row_key, 2), (), jnp.float32, math.log(scale_lo), math.log(scale_hi)))
        aligned = jnp.logical_or(jax.random.randint(jax.random.fold_in(couple_key, 1), (), 0, 100) < aligned_pct, index // 2 == chosen)
        ranks = jax.random.randint(jax.random.fold_in(couple_key, 2), (ND // 2,), 0, 1 << 20) + twinned * (1 << 21)
        target_couple = jnp.argmax(ranks).astype(jnp.int32)
        partner = data_row(shared, 2 * target_couple + index % 2, bound, scale_lo, scale_hi, twin_pct)
        exact = jax.random.randint(jax.random.fold_in(row_key, 3), (), 0, 100) < exact_pct
        strength = jnp.where(exact, 1.0, jax.random.uniform(jax.random.fold_in(row_key, 4), (), jnp.float32, strength_lo, strength_hi))
        remainder = jnp.sqrt(jnp.maximum(1.0 - strength * strength, 0.0))
        return jnp.where(aligned, strength * partner + remainder * spread * own, spread * own)
    rows = lax.map(one_row, jnp.arange(NN, dtype=jnp.int32))
    return rows.astype(jnp.bfloat16)


def setup_inputs(seed: int = 0) -> dict:
    arg_keys = jax.random.split(jax.random.key(seed), 3)
    noise_latents = draw_noise_latents(jax.random.fold_in(arg_keys[2], 71), 0)
    data_latents = draw_data_latents(jax.random.fold_in(arg_keys[2], 71), 0)
    return {"noise_latents": noise_latents, "data_latents": data_latents}


eps = 0.01


def logsumexp_axis(values, axis):
    peak = jnp.max(values, axis=axis, keepdims=True)
    total = jnp.sum(jnp.exp(values - peak), axis=axis)
    return jnp.squeeze(peak, axis) + jnp.log(total)


def reference(noise_latents, data_latents):
    noise_sq = jnp.sum(jnp.square(noise_latents.astype(jnp.float32)), axis=1)
    data_sq = jnp.sum(jnp.square(data_latents.astype(jnp.float32)), axis=1)
    inner = lax.dot_general(data_latents, noise_latents, (((1,), (1,)), ((), ())), preferred_element_type=jnp.float32)
    cost = (data_sq[:, None] + noise_sq[None, :] - 2.0 * inner) / F
    log_a = -math.log(NN)
    log_b = -math.log(ND)
    noise_pot = jnp.zeros((NN,), jnp.float32)
    data_pot = jnp.zeros((ND,), jnp.float32)
    for step in range(ITERS):
        noise_pot = eps * log_a - eps * logsumexp_axis((data_pot[:, None] - cost) / eps, 0)
        data_pot = eps * log_b - eps * logsumexp_axis((noise_pot[None, :] - cost) / eps, 1)
    plan = jnp.exp((noise_pot[None, :] + data_pot[:, None] - cost) / eps).astype(jnp.bfloat16)
    mass = jnp.sum(plan.astype(jnp.float32), axis=0)
    moved = lax.dot_general(plan, data_latents, (((0,), (0,)), ((), ())), preferred_element_type=jnp.float32)
    targets = (moved / mass[:, None]).astype(jnp.bfloat16)
    return targets, noise_pot, data_pot
```

```python
import functools
import math

import jax
import jax.numpy as jnp
from jax import lax
from jax.experimental import pallas as pl
from jax.experimental.pallas import tpu as pltpu
from jax.sharding import Mesh
from jax.sharding import PartitionSpec as P

F = 65536
ITERS = 4
eps = 0.01

NOISE = ("zl", "x")
PLANE = ("zh", "y")
DP = ("zh", "y", "c")
LANES = 128
BLOCKS = 4
CHUNK = 512
VMEM = pl.BlockSpec(memory_space=pltpu.VMEM)
SMEM = pl.BlockSpec(memory_space=pltpu.SMEM)
ANY = pl.BlockSpec(memory_space=pl.ANY)
f32 = jnp.float32


def params(mib):
    return pltpu.CompilerParams(vmem_limit_bytes=mib << 20)


def square_sums(ref):
    total = jnp.zeros((ref.shape[0], LANES), f32)
    for start in range(0, ref.shape[1], LANES):
        part = ref[:, start : start + LANES].astype(f32)
        total += part * part
    return jnp.sum(total, axis=1, keepdims=True)


def tile_kernel(place, *refs):
    noise, data = refs[:BLOCKS], refs[BLOCKS : BLOCKS + 6]
    sent, kept, whole, tall, wide, tall_sem, wide_sem, whole_sem = refs[BLOCKS + 6 :]
    rows = noise[0].shape[0]
    sub = kept.shape[2]

    def load_noise(k):
        return pltpu.make_async_copy(noise[k], tall.at[k], tall_sem.at[k])

    def load_data(ref, b):
        return pltpu.make_async_copy(ref, wide.at[b], wide_sem.at[b])

    for ref, step in [(data[k], step) for k, step in enumerate((0, -1, 1, -2, 2, 3))] + [(data[5], -3)]:
        block = place[1] + step

        @pl.when((block >= 0) & (block < BLOCKS))
        def _():
            load_data(ref, block).start()

    for k in range(BLOCKS):
        load_noise(k).start()
    for b in range(BLOCKS):
        load_data(data[0], b).wait()
    store = pltpu.make_async_copy(wide, whole, whole_sem)
    store.start()

    noise_sq = []
    for k in range(BLOCKS):
        load_noise(k).wait()
        noise_sq.append(square_sums(tall.at[k]))
    for out, half in ((sent, 1 - place[2]), (kept, place[2])):
        for b in range(BLOCKS // 2):
            block = half * (BLOCKS // 2) + b
            data_sq = jnp.broadcast_to(square_sums(wide.at[block]), (rows, LANES)).T[0:1]
            for k in range(BLOCKS):
                inner = lax.dot_general(tall[k], wide[block], (((1,), (1,)), ((), ())), preferred_element_type=f32)
                value = noise_sq[k] + data_sq - 2.0 * inner
                slot = lax.rem(place[0] + BLOCKS - k, BLOCKS)
                out[:, slot, :, b * rows : (b + 1) * rows] = value.reshape(rows // sub, sub, rows)
    store.wait()


def tile(place, noise, data, plane):
    rows, feats = data[0].shape
    dtype = data[0].dtype
    out = jax.ShapeDtypeStruct((plane, BLOCKS, rows // plane, BLOCKS // 2 * rows), f32)
    return pl.pallas_call(
        tile_kernel,
        out_shape=(out, out, jax.ShapeDtypeStruct((BLOCKS, rows, feats), dtype)),
        in_specs=[SMEM] + [ANY] * (BLOCKS + 6),
        out_specs=(VMEM, VMEM, ANY),
        scratch_shapes=[
            pltpu.VMEM((BLOCKS, rows, feats), dtype),
            pltpu.VMEM((BLOCKS, rows, feats), dtype),
            pltpu.SemaphoreType.DMA((BLOCKS,)),
            pltpu.SemaphoreType.DMA((BLOCKS,)),
            pltpu.SemaphoreType.DMA,
        ],
        compiler_params=params(56),
    )(place, *noise, *data)


def half_steps(cost, data_pot, log_a, local):
    blocks, rows, lanes = cost.shape

    def shifted(b):
        return -cost[b] if data_pot is None else data_pot[b : b + 1] - cost[b]

    peak = shifted(0)
    for b in range(1, blocks):
        peak = jnp.maximum(peak, shifted(b))
    peak = jnp.max(peak, axis=1, keepdims=True)
    total = jnp.exp(shifted(0) - peak)
    for b in range(1, blocks):
        total += jnp.exp(shifted(b) - peak)
    noise_pot = log_a - (peak + jnp.log(jnp.sum(total, axis=1, keepdims=True)))
    for b in range(blocks):
        value = noise_pot - cost[b]
        top = jnp.max(value, axis=0, keepdims=True)
        local[0, b : b + 1, :] = top + jnp.log(jnp.sum(jnp.exp(value - top), axis=0, keepdims=True))
    for k in range(1, local.shape[0]):
        local[k] = local[0]
    return noise_pot


def merge(everyone, log_b):
    peak = everyone[0]
    for k in range(1, everyone.shape[0]):
        peak = jnp.maximum(peak, everyone[k])
    total = jnp.exp(everyone[0] - peak)
    for k in range(1, everyone.shape[0]):
        total += jnp.exp(everyone[k] - peak)
    return log_b - (peak + jnp.log(total))


def first_kernel(log_a, place, mine, other, cost, local):
    xs, rows, width = mine.shape
    per_half = width // LANES
    for ref, half in ((mine, place[2]), (other, 1 - place[2])):
        for b in range(xs):
            for q in range(per_half):
                cost[b * BLOCKS + half * per_half + q] = ref[b, :, q * LANES : (q + 1) * LANES]
    half_steps(cost, None, log_a, local)


def middle_kernel(log_a, log_b, cost, everyone, local, noise_pot):
    noise_pot[...] = half_steps(cost, merge(everyone, log_b), log_a, local)


def last_kernel(log_b, place, cost, everyone, noise_pot, whole, targets, noise_out, data_out, pots, plan, data, sems):
    blocks, rows, lanes = cost.shape
    loads = []
    for n in range(targets.shape[1] // CHUNK):
        cols = pl.ds(n * CHUNK, CHUNK)
        loads.append(pltpu.make_async_copy(whole.at[:, cols], data.at[:, cols], sems.at[n]))
        loads[-1].start()

    pots[...] = merge(everyone, log_b)
    scaled = noise_pot[...]
    total = jnp.zeros((rows, lanes), f32)
    for b in range(blocks):
        entry = jnp.exp(scaled + pots[b : b + 1] - cost[b]).astype(jnp.bfloat16)
        total += entry.astype(f32)
        plan[:, b * lanes : (b + 1) * lanes] = entry
    mass = jnp.sum(total, axis=1, keepdims=True)
    noise_out[...] = jnp.broadcast_to(scaled * eps, (rows, lanes)).T[0:1]
    size = data_out.shape[1]
    row = pots[pl.ds(place[3], 1)] * eps
    mine = row[:, :size]
    for k in range(1, lanes // size):
        mine = jnp.where(place[4] == k, row[:, k * size : (k + 1) * size], mine)
    data_out[...] = mine

    for n, load in enumerate(loads):
        load.wait()
        cols = slice(n * CHUNK, (n + 1) * CHUNK)
        moved = jnp.dot(plan[...], data[:, cols], preferred_element_type=f32)
        targets[:, cols] = (moved / mass).astype(jnp.bfloat16)


def shards(noise_latents, data_latents):
    rows, feats = noise_latents.shape
    zl, x, zh, y, c = (lax.axis_size(a) for a in ("zl", "x", "zh", "y", "c"))
    plane = zh * y
    peers = zl * x
    total = peers * rows
    core, xi, zi = (lax.axis_index(a) for a in ("c", "x", "zl"))
    swap = [(0, 1), (1, 0)]

    owner = (lax.axis_index("zh") * y + lax.axis_index("y")) * c + core
    size = total // (plane * c)
    parts = rows // size
    block = owner // parts
    place = jnp.stack([xi, zi, core, (block % x) * zl + block // x, owner % parts])

    def send(value, axis, pairs):
        return lax.ppermute(value, axis, pairs)

    def turn(value, steps):
        return send(value, "x", [(i, (i + steps) % x) for i in range(x)])

    ups = [(i, i + 1) for i in range(zl - 1)]
    downs = [(i + 1, i) for i in range(zl - 1)]
    up, down = send(data_latents, "zl", ups), send(data_latents, "zl", downs)
    near = [turn(noise_latents, 1), turn(noise_latents, x - 1)]
    up, down, later_data, later_noise = lax.optimization_barrier((up, down, data_latents, noise_latents))
    up2, down2 = send(up, "zl", ups[1:]), send(down, "zl", downs[:-1])
    ends = send(later_data, "zl", [(0, zl - 1), (zl - 1, 0)])
    noise = [noise_latents, near[0], turn(later_noise, 2), near[1]]
    data = [data_latents, up, down, up2, down2, ends]

    sent, kept, whole = tile(place, noise, data, plane)
    came = lax.ppermute(sent, "c", swap)
    data_all = lax.all_gather(whole, "x").reshape(total, feats)
    pieces = lax.all_to_all(kept + came, PLANE, 0, 0, tiled=True)
    piece = jnp.sum(pieces, axis=0) / F / eps

    sub, half = piece.shape[1:]
    copies = jnp.broadcast_to(piece[:, None], (x, plane, sub, half)).reshape(x * plane, sub, half)
    mine = lax.all_to_all(copies, ("x",) + PLANE, 0, 0, tiled=True).reshape(x, rows, half)
    other = lax.ppermute(mine, "c", swap)

    log_a = log_b = -math.log(total)
    blocks = total // LANES
    exchanged = jax.ShapeDtypeStruct((peers, blocks, LANES), f32)
    column = jax.ShapeDtypeStruct((rows, 1), f32)
    cost, local = pl.pallas_call(
        functools.partial(first_kernel, log_a),
        out_shape=(jax.ShapeDtypeStruct((blocks, rows, LANES), f32), exchanged),
        in_specs=[SMEM, VMEM, VMEM],
        out_specs=(VMEM, VMEM),
        compiler_params=params(8),
    )(place, mine, other)
    for step in range(1, ITERS):
        everyone = lax.all_to_all(local, NOISE, 0, 0, tiled=True)
        local, noise_pot = pl.pallas_call(
            functools.partial(middle_kernel, log_a, log_b),
            out_shape=(exchanged, column),
            in_specs=[VMEM, VMEM],
            out_specs=(VMEM, VMEM),
            compiler_params=params(8),
        )(cost, everyone)
    everyone = lax.all_to_all(local, NOISE, 0, 0, tiled=True)

    targets, noise_out, data_out = pl.pallas_call(
        functools.partial(last_kernel, log_b),
        out_shape=(
            jax.ShapeDtypeStruct((rows, feats), jnp.bfloat16),
            jax.ShapeDtypeStruct((1, rows), f32),
            jax.ShapeDtypeStruct((1, size), f32),
        ),
        in_specs=[SMEM, VMEM, VMEM, VMEM] + [ANY],
        out_specs=(VMEM,) * 3,
        scratch_shapes=[
            pltpu.VMEM((blocks, LANES), f32),
            pltpu.VMEM((rows, total), jnp.bfloat16),
            pltpu.VMEM((total, feats), jnp.bfloat16),
            pltpu.SemaphoreType.DMA((feats // CHUNK,)),
        ],
        compiler_params=params(53),
    )(place, cost, everyone, noise_pot, data_all)
    return targets, noise_out[0], data_out[0]


def solution(mesh):
    fine = Mesh(mesh.devices.reshape(4, 4, 2, 8, 2), ("zl", "x", "zh", "y", "c"))
    placed = (P(NOISE, DP), P(NOISE, DP))
    return jax.shard_map(
        shards,
        mesh=fine,
        in_specs=placed,
        out_specs=(P(NOISE, DP), P(NOISE), P(DP)),
        check_vma=False,
    )
```

```python
import functools
import math

import jax
import jax.numpy as jnp
from jax import lax
from jax.experimental import pallas as pl
from jax.experimental.pallas import tpu as pltpu
from jax.sharding import Mesh
from jax.sharding import PartitionSpec as P

F = 65536
ITERS = 4
eps = 0.01

NOISE = ("zl", "x")
PLANE = ("zh", "y")
DP = ("zh", "y", "c")
LANES = 128
BLOCKS = 4
CHUNK = 512
VMEM = pl.BlockSpec(memory_space=pltpu.VMEM)
SMEM = pl.BlockSpec(memory_space=pltpu.SMEM)
ANY = pl.BlockSpec(memory_space=pl.ANY)
f32 = jnp.float32


def params(mib):
    return pltpu.CompilerParams(vmem_limit_bytes=mib << 20)


def square_sums(ref):
    total = jnp.zeros((ref.shape[0], LANES), f32)
    for start in range(0, ref.shape[1], LANES):
        part = ref[:, start : start + LANES].astype(f32)
        total += part * part
    return jnp.sum(total, axis=1, keepdims=True)


def tile_kernel(place, *refs):
    noise, data = refs[:BLOCKS], refs[BLOCKS : BLOCKS + 6]
    sent, kept, whole, tall, wide, tall_sem, wide_sem, whole_sem = refs[BLOCKS + 6 :]
    rows = noise[0].shape[0]
    sub = kept.shape[2]

    def load_noise(k):
        start = pl.multiple_of(lax.rem(place[0] + BLOCKS - k, BLOCKS) * rows, rows)
        return pltpu.make_async_copy(noise[k], tall.at[pl.ds(start, rows)], tall_sem.at[k])

    def load_data(ref, b):
        start = pl.multiple_of(b * rows, rows)
        return pltpu.make_async_copy(ref, wide.at[pl.ds(start, rows)], wide_sem.at[b])

    for ref, step in [(data[k], step) for k, step in enumerate((0, -1, 1, -2, 2, 3))] + [(data[5], -3)]:
        block = place[1] + step

        @pl.when((block >= 0) & (block < BLOCKS))
        def _():
            load_data(ref, block).start()

    for k in range(BLOCKS):
        load_noise(k).start()
    for b in range(BLOCKS):
        load_data(data[0], b).wait()
    store = pltpu.make_async_copy(wide, whole, whole_sem)
    store.start()

    for k in range(BLOCKS):
        load_noise(k).wait()
    noise_sq = square_sums(tall)
    half_rows = BLOCKS // 2 * rows
    for out, half in ((sent, 1 - place[2]), (kept, place[2])):
        block = wide.at[pl.ds(pl.multiple_of(half * half_rows, half_rows), half_rows)]
        data_sq = jnp.broadcast_to(square_sums(block), (half_rows, LANES)).T[0:1]
        inner = lax.dot_general(tall[...], block[...], (((1,), (1,)), ((), ())), preferred_element_type=f32)
        value = noise_sq + data_sq - 2.0 * inner
        for slot in range(BLOCKS):
            out[:, slot] = value[slot * rows : (slot + 1) * rows].reshape(rows // sub, sub, half_rows)
    store.wait()


def tile(place, noise, data, plane):
    rows, feats = data[0].shape
    dtype = data[0].dtype
    out = jax.ShapeDtypeStruct((plane, BLOCKS, rows // plane, BLOCKS // 2 * rows), f32)
    return pl.pallas_call(
        tile_kernel,
        out_shape=(out, out, jax.ShapeDtypeStruct((BLOCKS * rows, feats), dtype)),
        in_specs=[SMEM] + [ANY] * (BLOCKS + 6),
        out_specs=(VMEM, VMEM, ANY),
        scratch_shapes=[
            pltpu.VMEM((BLOCKS * rows, feats), dtype),
            pltpu.VMEM((BLOCKS * rows, feats), dtype),
            pltpu.SemaphoreType.DMA((BLOCKS,)),
            pltpu.SemaphoreType.DMA((BLOCKS,)),
            pltpu.SemaphoreType.DMA,
        ],
        compiler_params=params(56),
    )(place, *noise, *data)


def half_steps(cost, data_pot, log_a, local):
    blocks, rows, lanes = cost.shape

    def shifted(b):
        return -cost[b] if data_pot is None else data_pot[b : b + 1] - cost[b]

    peak = shifted(0)
    for b in range(1, blocks):
        peak = jnp.maximum(peak, shifted(b))
    peak = jnp.max(peak, axis=1, keepdims=True)
    total = jnp.exp(shifted(0) - peak)
    for b in range(1, blocks):
        total += jnp.exp(shifted(b) - peak)
    noise_pot = log_a - (peak + jnp.log(jnp.sum(total, axis=1, keepdims=True)))
    for b in range(blocks):
        value = noise_pot - cost[b]
        top = jnp.max(value, axis=0, keepdims=True)
        local[0, b : b + 1, :] = top + jnp.log(jnp.sum(jnp.exp(value - top), axis=0, keepdims=True))
    for k in range(1, local.shape[0]):
        local[k] = local[0]
    return noise_pot


def merge(everyone, log_b):
    peak = everyone[0]
    for k in range(1, everyone.shape[0]):
        peak = jnp.maximum(peak, everyone[k])
    total = jnp.exp(everyone[0] - peak)
    for k in range(1, everyone.shape[0]):
        total += jnp.exp(everyone[k] - peak)
    return log_b - (peak + jnp.log(total))


def first_kernel(log_a, place, mine, other, cost, local):
    xs, rows, width = mine.shape
    per_half = width // LANES
    for ref, half in ((mine, place[2]), (other, 1 - place[2])):
        for b in range(xs):
            for q in range(per_half):
                cost[b * BLOCKS + half * per_half + q] = ref[b, :, q * LANES : (q + 1) * LANES]
    half_steps(cost, None, log_a, local)


def middle_kernel(log_a, log_b, cost, everyone, local, noise_pot):
    noise_pot[...] = half_steps(cost, merge(everyone, log_b), log_a, local)


def last_kernel(log_b, place, cost, everyone, noise_pot, whole, targets, noise_out, data_out, pots, plan, data, sems):
    blocks, rows, lanes = cost.shape
    loads = []
    for n in range(targets.shape[1] // CHUNK):
        cols = pl.ds(n * CHUNK, CHUNK)
        loads.append(pltpu.make_async_copy(whole.at[:, cols], data.at[:, cols], sems.at[n]))
        loads[-1].start()

    pots[...] = merge(everyone, log_b)
    scaled = noise_pot[...]
    total = jnp.zeros((rows, lanes), f32)
    for b in range(blocks):
        entry = jnp.exp(scaled + pots[b : b + 1] - cost[b]).astype(jnp.bfloat16)
        total += entry.astype(f32)
        plan[:, b * lanes : (b + 1) * lanes] = entry
    mass = jnp.sum(total, axis=1, keepdims=True)
    noise_out[...] = jnp.broadcast_to(scaled * eps, (rows, lanes)).T[0:1]
    size = data_out.shape[1]
    row = pots[pl.ds(place[3], 1)] * eps
    mine = row[:, :size]
    for k in range(1, lanes // size):
        mine = jnp.where(place[4] == k, row[:, k * size : (k + 1) * size], mine)
    data_out[...] = mine

    for n, load in enumerate(loads):
        load.wait()
        cols = slice(n * CHUNK, (n + 1) * CHUNK)
        moved = jnp.dot(plan[...], data[:, cols], preferred_element_type=f32)
        targets[:, cols] = (moved / mass).astype(jnp.bfloat16)


def shards(noise_latents, data_latents):
    rows, feats = noise_latents.shape
    zl, x, zh, y, c = (lax.axis_size(a) for a in ("zl", "x", "zh", "y", "c"))
    plane = zh * y
    peers = zl * x
    total = peers * rows
    core, xi, zi = (lax.axis_index(a) for a in ("c", "x", "zl"))
    swap = [(0, 1), (1, 0)]

    owner = (lax.axis_index("zh") * y + lax.axis_index("y")) * c + core
    size = total // (plane * c)
    parts = rows // size
    block = owner // parts
    place = jnp.stack([xi, zi, core, (block % x) * zl + block // x, owner % parts])

    def send(value, axis, pairs):
        return lax.ppermute(value, axis, pairs)

    def turn(value, steps):
        return send(value, "x", [(i, (i + steps) % x) for i in range(x)])

    ups = [(i, i + 1) for i in range(zl - 1)]
    downs = [(i + 1, i) for i in range(zl - 1)]
    up, down = send(data_latents, "zl", ups), send(data_latents, "zl", downs)
    ends = send(data_latents, "zl", [(0, zl - 1), (zl - 1, 0)])
    noise = [noise_latents] + [turn(noise_latents, k) for k in range(1, x - 1)]
    up2, down2 = send(up, "zl", ups[1:]), send(down, "zl", downs[:-1])
    later, *_ = lax.optimization_barrier((noise_latents, up, down))
    noise.append(turn(later, x - 1))
    data = [data_latents, up, down, up2, down2, ends]

    sent, kept, whole = tile(place, noise, data, plane)
    came = lax.ppermute(sent, "c", swap)
    data_all = lax.all_gather(whole, "x").reshape(total, feats)
    pieces = lax.all_to_all(kept + came, PLANE, 0, 0, tiled=True)
    piece = jnp.sum(pieces, axis=0) / F / eps

    sub, half = piece.shape[1:]
    copies = jnp.broadcast_to(piece[:, None], (x, plane, sub, half)).reshape(x * plane, sub, half)
    mine = lax.all_to_all(copies, ("x",) + PLANE, 0, 0, tiled=True).reshape(x, rows, half)
    other = lax.ppermute(mine, "c", swap)

    log_a = log_b = -math.log(total)
    blocks = total // LANES
    exchanged = jax.ShapeDtypeStruct((peers, blocks, LANES), f32)
    column = jax.ShapeDtypeStruct((rows, 1), f32)
    cost, local = pl.pallas_call(
        functools.partial(first_kernel, log_a),
        out_shape=(jax.ShapeDtypeStruct((blocks, rows, LANES), f32), exchanged),
        in_specs=[SMEM, VMEM, VMEM],
        out_specs=(VMEM, VMEM),
        compiler_params=params(8),
    )(place, mine, other)
    for step in range(1, ITERS):
        everyone = lax.all_to_all(local, NOISE, 0, 0, tiled=True)
        local, noise_pot = pl.pallas_call(
            functools.partial(middle_kernel, log_a, log_b),
            out_shape=(exchanged, column),
            in_specs=[VMEM, VMEM],
            out_specs=(VMEM, VMEM),
            compiler_params=params(8),
        )(cost, everyone)
    everyone = lax.all_to_all(local, NOISE, 0, 0, tiled=True)

    targets, noise_out, data_out = pl.pallas_call(
        functools.partial(last_kernel, log_b),
        out_shape=(
            jax.ShapeDtypeStruct((rows, feats), jnp.bfloat16),
            jax.ShapeDtypeStruct((1, rows), f32),
            jax.ShapeDtypeStruct((1, size), f32),
        ),
        in_specs=[SMEM, VMEM, VMEM, VMEM] + [ANY],
        out_specs=(VMEM,) * 3,
        scratch_shapes=[
            pltpu.VMEM((blocks, LANES), f32),
            pltpu.VMEM((rows, total), jnp.bfloat16),
            pltpu.VMEM((total, feats), jnp.bfloat16),
            pltpu.SemaphoreType.DMA((feats // CHUNK,)),
        ],
        compiler_params=params(53),
    )(place, cost, everyone, noise_pot, data_all)
    return targets, noise_out[0], data_out[0]


def solution(mesh):
    fine = Mesh(mesh.devices.reshape(4, 4, 2, 8, 2), ("zl", "x", "zh", "y", "c"))
    placed = (P(NOISE, DP), P(NOISE, DP))
    return jax.shard_map(
        shards,
        mesh=fine,
        in_specs=placed,
        out_specs=(P(NOISE, DP), P(NOISE), P(DP)),
        check_vma=False,
    )
```

```python
import functools
import math

import jax
import jax.numpy as jnp
from jax import lax
from jax.experimental import pallas as pl
from jax.experimental.pallas import tpu as pltpu
from jax.sharding import Mesh
from jax.sharding import PartitionSpec as P

F = 65536
ITERS = 4
eps = 0.01

NOISE = ("zl", "x")
PLANE = ("zh", "y")
DP = ("zh", "y", "c")
LANES = 128
BLOCKS = 4
CHUNK = 512
VMEM = pl.BlockSpec(memory_space=pltpu.VMEM)
SMEM = pl.BlockSpec(memory_space=pltpu.SMEM)
ANY = pl.BlockSpec(memory_space=pl.ANY)
f32 = jnp.float32


def params(mib):
    return pltpu.CompilerParams(vmem_limit_bytes=mib << 20)


def square_sums(ref):
    total = jnp.zeros((ref.shape[0], LANES), f32)
    for start in range(0, ref.shape[1], LANES):
        part = ref[:, start : start + LANES].astype(f32)
        total += part * part
    return jnp.sum(total, axis=1, keepdims=True)


def tile_kernel(place, *refs):
    noise, data = refs[:BLOCKS], refs[BLOCKS : BLOCKS + 6]
    sent, kept, whole, tall, wide, tall_sem, wide_sem, whole_sem = refs[BLOCKS + 6 :]
    rows = noise[0].shape[0]
    sub = kept.shape[2]

    def load_noise(k):
        start = pl.multiple_of(lax.rem(place[0] + BLOCKS - k, BLOCKS) * rows, rows)
        return pltpu.make_async_copy(noise[k], tall.at[pl.ds(start, rows)], tall_sem.at[k])

    def load_data(ref, b):
        start = pl.multiple_of(b * rows, rows)
        return pltpu.make_async_copy(ref, wide.at[pl.ds(start, rows)], wide_sem.at[b])

    for ref, step in [(data[k], step) for k, step in enumerate((0, -1, 1, -2, 2, 3))] + [(data[5], -3)]:
        block = place[1] + step

        @pl.when((block >= 0) & (block < BLOCKS))
        def _():
            load_data(ref, block).start()

    for k in range(BLOCKS):
        load_noise(k).start()
    for b in range(BLOCKS):
        load_data(data[0], b).wait()
    store = pltpu.make_async_copy(wide, whole, whole_sem)
    store.start()

    for k in range(BLOCKS):
        load_noise(k).wait()
    noise_sq = square_sums(tall)
    half_rows = BLOCKS // 2 * rows
    for out, half in ((sent, 1 - place[2]), (kept, place[2])):
        block = wide.at[pl.ds(pl.multiple_of(half * half_rows, half_rows), half_rows)]
        data_sq = jnp.broadcast_to(square_sums(block), (half_rows, LANES)).T[0:1]
        inner = lax.dot_general(tall[...], block[...], (((1,), (1,)), ((), ())), preferred_element_type=f32)
        value = noise_sq + data_sq - 2.0 * inner
        for slot in range(BLOCKS):
            out[:, slot] = value[slot * rows : (slot + 1) * rows].reshape(rows // sub, sub, half_rows)
    store.wait()


def tile(place, noise, data, plane):
    rows, feats = data[0].shape
    dtype = data[0].dtype
    out = jax.ShapeDtypeStruct((plane, BLOCKS, rows // plane, BLOCKS // 2 * rows), f32)
    return pl.pallas_call(
        tile_kernel,
        out_shape=(out, out, jax.ShapeDtypeStruct((BLOCKS * rows, feats), dtype)),
        in_specs=[SMEM] + [ANY] * (BLOCKS + 6),
        out_specs=(VMEM, VMEM, ANY),
        scratch_shapes=[
            pltpu.VMEM((BLOCKS * rows, feats), dtype),
            pltpu.VMEM((BLOCKS * rows, feats), dtype),
            pltpu.SemaphoreType.DMA((BLOCKS,)),
            pltpu.SemaphoreType.DMA((BLOCKS,)),
            pltpu.SemaphoreType.DMA,
        ],
        compiler_params=params(56),
    )(place, *noise, *data)


def half_steps(cost, data_pot, log_a, local):
    blocks, rows, lanes = cost.shape

    def shifted(b):
        return -cost[b] if data_pot is None else data_pot[b : b + 1] - cost[b]

    peak = shifted(0)
    for b in range(1, blocks):
        peak = jnp.maximum(peak, shifted(b))
    peak = jnp.max(peak, axis=1, keepdims=True)
    total = jnp.exp(shifted(0) - peak)
    for b in range(1, blocks):
        total += jnp.exp(shifted(b) - peak)
    noise_pot = log_a - (peak + jnp.log(jnp.sum(total, axis=1, keepdims=True)))
    for b in range(blocks):
        value = noise_pot - cost[b]
        top = jnp.max(value, axis=0, keepdims=True)
        local[0, b : b + 1, :] = top + jnp.log(jnp.sum(jnp.exp(value - top), axis=0, keepdims=True))
    for k in range(1, local.shape[0]):
        local[k] = local[0]
    return noise_pot


def merge(everyone, log_b):
    peak = everyone[0]
    for k in range(1, everyone.shape[0]):
        peak = jnp.maximum(peak, everyone[k])
    total = jnp.exp(everyone[0] - peak)
    for k in range(1, everyone.shape[0]):
        total += jnp.exp(everyone[k] - peak)
    return log_b - (peak + jnp.log(total))


def first_kernel(log_a, place, mine, other, cost, local):
    xs, rows, width = mine.shape
    per_half = width // LANES
    for ref, half in ((mine, place[2]), (other, 1 - place[2])):
        for b in range(xs):
            for q in range(per_half):
                cost[b * BLOCKS + half * per_half + q] = ref[b, :, q * LANES : (q + 1) * LANES]
    half_steps(cost, None, log_a, local)


def middle_kernel(log_a, log_b, cost, everyone, local, *noise_out):
    noise_pot = half_steps(cost, merge(everyone, log_b), log_a, local)
    for ref in noise_out:
        ref[...] = noise_pot


def last_kernel(log_b, place, cost, everyone, noise_pot, whole, targets, noise_out, data_out, pots, plan, data, sems):
    blocks, rows, lanes = cost.shape
    loads = []
    for n in range(targets.shape[1] // CHUNK):
        cols = pl.ds(n * CHUNK, CHUNK)
        loads.append(pltpu.make_async_copy(whole.at[:, cols], data.at[:, cols], sems.at[n]))
        loads[-1].start()

    pots[...] = merge(everyone, log_b)
    scaled = noise_pot[...]
    total = jnp.zeros((rows, lanes), f32)
    for b in range(blocks):
        entry = jnp.exp(scaled + pots[b : b + 1] - cost[b]).astype(jnp.bfloat16)
        total += entry.astype(f32)
        plan[:, b * lanes : (b + 1) * lanes] = entry
    mass = jnp.sum(total, axis=1, keepdims=True)
    noise_out[...] = jnp.broadcast_to(scaled * eps, (rows, lanes)).T[0:1]
    size = data_out.shape[1]
    row = pots[pl.ds(place[3], 1)] * eps
    mine = row[:, :size]
    for k in range(1, lanes // size):
        mine = jnp.where(place[4] == k, row[:, k * size : (k + 1) * size], mine)
    data_out[...] = mine

    for n, load in enumerate(loads):
        load.wait()
        cols = slice(n * CHUNK, (n + 1) * CHUNK)
        moved = jnp.dot(plan[...], data[:, cols], preferred_element_type=f32)
        targets[:, cols] = (moved / mass).astype(jnp.bfloat16)


def shards(noise_latents, data_latents):
    rows, feats = noise_latents.shape
    zl, x, zh, y, c = (lax.axis_size(a) for a in ("zl", "x", "zh", "y", "c"))
    plane = zh * y
    peers = zl * x
    total = peers * rows
    core, xi, zi = (lax.axis_index(a) for a in ("c", "x", "zl"))
    swap = [(0, 1), (1, 0)]

    owner = (lax.axis_index("zh") * y + lax.axis_index("y")) * c + core
    size = total // (plane * c)
    parts = rows // size
    block = owner // parts
    place = jnp.stack([xi, zi, core, (block % x) * zl + block // x, owner % parts])

    def send(value, axis, pairs):
        return lax.ppermute(value, axis, pairs)

    def turn(value, steps):
        return send(value, "x", [(i, (i + steps) % x) for i in range(x)])

    ups = [(i, i + 1) for i in range(zl - 1)]
    downs = [(i + 1, i) for i in range(zl - 1)]
    up, down = send(data_latents, "zl", ups), send(data_latents, "zl", downs)
    ends = send(data_latents, "zl", [(0, zl - 1), (zl - 1, 0)])
    noise = [noise_latents] + [turn(noise_latents, k) for k in range(1, x - 1)]
    up2, down2 = send(up, "zl", ups[1:]), send(down, "zl", downs[:-1])
    later, *_ = lax.optimization_barrier((noise_latents, up, down))
    noise.append(turn(later, x - 1))
    data = [data_latents, up, down, up2, down2, ends]

    sent, kept, whole = tile(place, noise, data, plane)
    came = lax.ppermute(sent, "c", swap)
    data_all = lax.all_gather(whole, "x").reshape(total, feats)
    pieces = lax.all_to_all(kept + came, PLANE, 0, 0, tiled=True)
    piece = jnp.sum(pieces, axis=0) / F / eps

    sub, half = piece.shape[1:]
    copies = jnp.broadcast_to(piece[:, None], (x, plane, sub, half)).reshape(x * plane, sub, half)
    mine = lax.all_to_all(copies, ("x",) + PLANE, 0, 0, tiled=True).reshape(x, rows, half)
    other = lax.ppermute(mine, "c", swap)

    log_a = log_b = -math.log(total)
    blocks = total // LANES
    exchanged = jax.ShapeDtypeStruct((peers, blocks, LANES), f32)
    column = jax.ShapeDtypeStruct((rows, 1), f32)
    cost, local = pl.pallas_call(
        functools.partial(first_kernel, log_a),
        out_shape=(jax.ShapeDtypeStruct((blocks, rows, LANES), f32), exchanged),
        in_specs=[SMEM, VMEM, VMEM],
        out_specs=(VMEM, VMEM),
        compiler_params=params(8),
    )(place, mine, other)
    for step in range(1, ITERS):
        everyone = lax.all_to_all(local, ("x", "zl"), 0, 0, tiled=True)
        shapes = (exchanged, column) if step == ITERS - 1 else (exchanged,)
        local, *noise_pot = pl.pallas_call(
            functools.partial(middle_kernel, log_a, log_b),
            out_shape=shapes,
            in_specs=[VMEM, VMEM],
            out_specs=(VMEM,) * len(shapes),
            compiler_params=params(8),
        )(cost, everyone)
    everyone = lax.all_to_all(local, ("x", "zl"), 0, 0, tiled=True)

    targets, noise_out, data_out = pl.pallas_call(
        functools.partial(last_kernel, log_b),
        out_shape=(
            jax.ShapeDtypeStruct((rows, feats), jnp.bfloat16),
            jax.ShapeDtypeStruct((1, rows), f32),
            jax.ShapeDtypeStruct((1, size), f32),
        ),
        in_specs=[SMEM, VMEM, VMEM, VMEM, ANY],
        out_specs=(VMEM,) * 3,
        scratch_shapes=[
            pltpu.VMEM((blocks, LANES), f32),
            pltpu.VMEM((rows, total), jnp.bfloat16),
            pltpu.VMEM((total, feats), jnp.bfloat16),
            pltpu.SemaphoreType.DMA((feats // CHUNK,)),
        ],
        compiler_params=params(53),
    )(place, cost, everyone, *noise_pot, data_all)
    return targets, noise_out[0], data_out[0]


def solution(mesh):
    fine = Mesh(mesh.devices.reshape(4, 4, 2, 8, 2), ("zl", "x", "zh", "y", "c"))
    placed = (P(NOISE, DP), P(NOISE, DP))
    return jax.shard_map(
        shards,
        mesh=fine,
        in_specs=placed,
        out_specs=(P(NOISE, DP), P(NOISE), P(DP)),
        check_vma=False,
    )
```
